256 devices in a mesh: aux: 16 (over x, y_lo, core), virt: 16 (over z, y_hi).
Axes of the slice: x: 4, y: 4 (y_hi: 2, y_lo: 2; y = y_hi * 2 + y_lo), z: 8, core: 2. Of those that a mesh axis runs over, the one named last changes fastest.
Arguments:
- orbital_block: bfloat16 [16384, 4096], P('aux', 'virt'), may hold values from -0.046875 to 0.046875
- partner_blocks: bfloat16 [1, 16384, 4096], P(None, 'aux', 'virt'), may hold values from -0.046875 to 0.046875
- occ_energy: float32 [2], replicated, may hold values from -2 to -0.3
- virt_energy: float32 [4096], replicated, may hold values from 0.2 to 3
Outputs:
- gamma_own: float32 [16384, 4096], P('aux', 'virt')
- gamma_partner: float32 [1, 16384, 4096], P(None, 'aux', 'virt')
The draws below stay inside these ranges and needn't reach their ends.
All inputs are finite; a program needn't handle non-finite values.
Results may differ from the reference program's by a relative error of at most 0.0038.
Values may be sent and summed in bfloat16 or wider, within the bound.
No kernel may reach another device: no remote copies, remote signals or barrier semaphores. Data moves between devices by JAX's collectives and lax.ppermute only.
A program may use at most 128 MiB of HBM per device.

```python
import jax
import jax.numpy as jnp
from jax import lax

NV = 4096
NAUX = 16384
PAIRS = 1
N_VIRT = 16


def level_of(own_key, dims, pieces, least, high):
    def one(position, parts):
        heights = jax.random.uniform(jax.random.fold_in(jax.random.fold_in(own_key, 6), position), (parts,), jnp.float32, least / len(pieces), high / len(pieces))
        return jnp.repeat(jnp.exp(heights), dims[position] // parts).reshape((-1,) + (1,) * (len(dims) - position - 1))

    level = one(*pieces[0])
    for cut in pieces[1:]:
        level = level * one(*cut)
    return level


def normal_values(key, shape, deviation, bound, shards=(), dtype=jnp.bfloat16):
    gain = level_of(key, shape, shards, -0.22, 0.18) if shards else 1.0
    array = jax.random.normal(key, shape, jnp.float32) * deviation * gain
    return jnp.minimum(jnp.maximum(array, -bound), bound).astype(dtype)


def setup_inputs(seed: int = 0) -> dict:
    seeds = jax.random.split(jax.random.key(seed), 5)
    return {
        "orbital_block": normal_values(seeds[0], (NAUX, NV), NAUX ** -0.5, 0.046875, ((0, 16), (1, 16))),
        "partner_blocks": normal_values(seeds[1], (PAIRS, NAUX, NV), NAUX ** -0.5, 0.046875, ((1, 16), (2, 16))),
        "occ_energy": jnp.clip(jax.random.uniform(seeds[2], (PAIRS + 1,), jnp.float32, -2.0, -0.3), -2.0, -0.3),
        "virt_energy": jnp.clip(jax.random.uniform(seeds[3], (NV,), jnp.float32, 0.2, 3.0), 0.2, 3.0),
    }


def reference(orbital_block, partner_blocks, occ_energy, virt_energy):
    own = orbital_block.astype(jnp.float32)
    gamma_own = jnp.zeros(own.shape, jnp.float32)
    block_width = NV // N_VIRT
    outputs = []
    for index in range(PAIRS):
        partner = partner_blocks[index].astype(jnp.float32)
        integrals = jnp.dot(own.T, partner, precision=lax.Precision.HIGHEST, preferred_element_type=jnp.float32)
        numerator = 2.0 * integrals - integrals.T
        denom = occ_energy[0] + occ_energy[index + 1] - virt_energy[:, None] - virt_energy[None, :]
        amplitudes = (numerator / denom).astype(jnp.bfloat16)
        amplitudes = lax.optimization_barrier(amplitudes).astype(jnp.float32)
        gamma_own = gamma_own + jnp.dot(partner, amplitudes.T, precision=lax.Precision.HIGHEST, preferred_element_type=jnp.float32)
        total = jnp.zeros((NAUX, NV), jnp.float32)
        for block in range(N_VIRT):
            lower = block * block_width
            piece = jnp.dot(own[:, lower:lower + block_width], amplitudes[lower:lower + block_width, :], precision=lax.Precision.HIGHEST, preferred_element_type=jnp.float32)
            piece = lax.optimization_barrier(piece.astype(jnp.bfloat16)).astype(jnp.float32)
            total = total + piece
        outputs.append(total)
    return gamma_own, jnp.stack(outputs)
```

```python
import functools

import jax
import jax.numpy as jnp
from jax import lax
from jax.experimental import pallas as pl
from jax.experimental.pallas import tpu as pltpu
from jax.sharding import Mesh, PartitionSpec as P

AXES = ("x", "yl", "c", "z", "yh")
SIZES = (4, 2, 2, 8, 2)
NZ = 8
CHIPS = 8
F32, BF16 = jnp.float32, jnp.bfloat16


def shift(value, axis, size, step):
    return lax.ppermute(value, axis, [(i, (i + step) % size) for i in range(size)])


def swap(value, axis):
    return lax.ppermute(value, axis, [(0, 1), (1, 0)])


class Lazy:
    def __init__(self, scratch, copy):
        self.scratch, self.copy = scratch, copy

    def get(self):
        if self.copy is not None:
            self.copy.wait()
            self.copy = None
        return self.scratch


def call(kernel, out_shape, *args, scalar=False):
    lead = 1 if scalar else 0
    moved = args[lead:]
    count = len(moved)
    outs = len(jax.tree.leaves(out_shape))

    def body(*refs):
        sources = refs[lead:lead + count]
        targets = refs[lead + count:lead + count + outs]
        scratch = refs[lead + count + outs:-1]
        sems = refs[-1]
        lazy = []
        for index in range(count):
            copy = pltpu.make_async_copy(sources[index], scratch[index], sems.at[index])
            copy.start()
            lazy.append(Lazy(scratch[index], copy))
        kernel(*refs[:lead], *lazy, *targets)
        for item in lazy:
            item.get()

    specs = [pl.BlockSpec(memory_space=pltpu.SMEM)] * lead + [pl.BlockSpec(memory_space=pltpu.HBM)] * count
    out_specs = jax.tree.map(lambda _: pl.BlockSpec(memory_space=pltpu.VMEM), out_shape)
    return pl.pallas_call(
        body,
        out_shape=out_shape,
        in_specs=specs,
        out_specs=out_specs,
        scratch_shapes=[pltpu.VMEM(arg.shape, arg.dtype) for arg in moved] + [pltpu.SemaphoreType.DMA((count,))],
        cost_estimate=pl.CostEstimate(flops=0, bytes_accessed=0, transcendentals=0),
        compiler_params=pltpu.CompilerParams(vmem_limit_bytes=56 * 1024 * 1024),
    )(*args)


def prepare_kernel(width, core, *refs):
    out = refs[-1]
    parts = [ref.get() for ref in refs[:-1]]
    count = len(parts) // 2
    zero = core[0] == 0
    start = 0
    for index in range(count):
        here, peer = parts[index], parts[count + index]
        rows = here.shape[0]
        for side in range(2):
            columns = slice(side * width, (side + 1) * width)
            first, second = here[:, columns].T, peer[:, columns].T
            into = slice(start, start + rows)
            out[2 * side * width:(2 * side + 1) * width, into] = jnp.where(zero, first, second)
            out[(2 * side + 1) * width:(2 * side + 2) * width, into] = jnp.where(zero, second, first)
        start += rows


def products_kernel(counts, width, *refs):
    left = refs[0].get()
    kept, given = refs[-2:]
    position = 1
    for index, count in enumerate(counts):
        parts = [ref.get() for ref in refs[position:position + count]]
        position += count
        for side in range(2):
            columns = slice(width, 2 * width) if side == 0 else slice(0, width)
            total = None
            start = 0
            for part in parts:
                rows = part.shape[0]
                value = jnp.dot(
                    left[2 * side * width:(2 * side + 2) * width, start:start + rows],
                    part[:, columns],
                    preferred_element_type=F32,
                )
                total = value if total is None else total + value
                start += rows
            place = slice((2 * index + side) * width, (2 * index + side + 1) * width)
            kept[:, place] = total[:width]
            given[:, place] = total[width:].astype(BF16)


def products(left, blocks, width):
    counts = [len(block) for block in blocks]
    flat = [part for block in blocks for part in block]
    shape = (width, 2 * width * len(blocks))
    shapes = (jax.ShapeDtypeStruct(shape, F32), jax.ShapeDtypeStruct(shape, BF16))
    return call(functools.partial(products_kernel, counts, width), shapes, left, *flat)


def amplitude_kernel(count, width, copies, pieces, row_level, col_energy, out):
    pieces, row_level, col_energy = pieces.get(), row_level.get(), col_energy.get()
    for index in range(count):
        denom = row_level[...] - col_energy[:, index * width:(index + 1) * width]
        direct = None
        crossed = None
        for chip in range(CHIPS):
            first = pieces[chip, :, (2 * index) * width:(2 * index + 1) * width].astype(F32)
            second = pieces[chip, :, (2 * index + 1) * width:(2 * index + 2) * width].astype(F32)
            direct = first if direct is None else direct + first
            crossed = second if crossed is None else crossed + second
        amp = ((2.0 * direct - crossed) / denom).astype(BF16)
        amp_crossed = ((2.0 * crossed - direct) / denom).astype(BF16)
        for copy in range(copies):
            out[copy, :, (2 * index) * width:(2 * index + 1) * width] = amp
            out[copy, :, (2 * index + 1) * width:(2 * index + 2) * width] = amp_crossed


def contract(block, amps):
    return lax.dot_general(block, amps, (((1,), (1,)), ((), ())), preferred_element_type=F32)


def gamma_kernel(count, width, step, side, add, *refs):
    core, mine, other = refs[0], refs[1].get(), refs[2].get()
    flat = [ref.get() for ref in refs[3:3 + 2 * count]]
    outs = refs[-2:]
    sums = [ref.get() for ref in refs[3 + 2 * count:5 + 2 * count]] if add else None
    zero = core[0] == 0
    columns = slice(width, 2 * width) if side == 0 else slice(0, width)
    for store in range(2):
        chosen = zero if store == 0 else jnp.logical_not(zero)
        amps = []
        for index in range(count):
            place = slice((2 * index + side) * width, (2 * index + side + 1) * width)
            amps.append(jnp.where(chosen, mine[:, place], other[:, place]))
        for part in range(2):
            size = flat[part].shape[0]
            for start in range(0, size, step):
                rows = slice(start, start + step)
                into = slice(part * size + start, part * size + start + step)
                total = None
                for index in range(count):
                    value = contract(flat[2 * index + part][rows, columns], amps[index])
                    total = value if total is None else total + value
                if add:
                    total = total + sums[store][into, :]
                outs[store][into, :] = total.astype(outs[store].dtype)


def local(own, partner_blocks, occ_energy, virt_energy):
    x, yl, c, z, yh = (lax.axis_index(name) for name in AXES)
    k = x * 2 + yl
    depth, width = own.shape
    half = depth // 2
    rows = width // CHIPS
    step = min(256, half)
    first = c == 0
    core = c.astype(jnp.int32).reshape(1)

    base = jnp.concatenate([own, partner_blocks[0]], axis=1)
    base = base[:half], base[half:]
    base_peer = tuple(swap(part, "yh") for part in base)
    shape = jax.ShapeDtypeStruct((4 * width, depth), BF16)
    left = call(functools.partial(prepare_kernel, width), shape, core, *base, *base_peer, scalar=True)
    level = occ_energy[0] + occ_energy[1]
    row_energy = lax.dynamic_slice_in_dim(virt_energy, (z * 2 + (yh ^ c)) * width + k * rows, rows)
    row_level = (level - row_energy)[:, None]
    by_block = virt_energy.reshape(NZ, 2, width)
    col_energy = {d: lax.dynamic_slice(by_block, ((z + d) % NZ, yh, 0), (1, 1, width)).reshape(1, width) for d in range(-3, 5)}

    def after(values, *others):
        return lax.optimization_barrier((values, others))[0]

    def combined(blocks):
        kept, given = products(left, blocks, width)
        return (kept + swap(given, "c").astype(F32)).astype(BF16).reshape(CHIPS, rows, -1)

    def scatter(summed):
        return lax.all_to_all(summed, ("x", "yl"), 0, 0, tiled=True)

    def amplitudes(group, pieces, copies):
        cols = jnp.concatenate([col_energy[d] for d in group], axis=1)
        shape = jax.ShapeDtypeStruct((copies, rows, 2 * width * len(group)), BF16)
        kernel = functools.partial(amplitude_kernel, len(group), width, copies)
        return call(kernel, shape, pieces, row_level, cols)

    def spread(copies):
        return lax.all_to_all(copies, ("x", "yl"), 0, 0, tiled=True).reshape(width, -1)

    def gamma(side, blocks, mine, other, sums):
        kernel = functools.partial(gamma_kernel, len(blocks), width, step, side, sums is not None)
        shape = (depth, width)
        shapes = jax.ShapeDtypeStruct(shape, F32), jax.ShapeDtypeStruct(shape, F32 if sums is None else BF16)
        flat = [part for block in blocks for part in block]
        return call(kernel, shapes, core, mine, other, *flat, *(sums or ()), scalar=True)

    def both(parts, way):
        return tuple(shift(part, "z", NZ, way) for part in parts)

    up1, down1 = both(base, 1), both(base, -1)
    up2, down2 = both(up1, 1), both(down1, -1)
    up3, down3 = both(up2, 1), both(down2, -1)
    far = shift(up3[0], "z", NZ, 1), shift(down3[1], "z", NZ, -1)

    near, distant = (0, 1, -1, 2, -2), (3, -3, 4)
    near_blocks, distant_blocks = [base, down1, up1, down2, up2], [down3, up3, far]
    pieces_a = scatter(after(combined(near_blocks), up3[0], down3[0]))
    amp_a = amplitudes(near, after(pieces_a, far), CHIPS)
    pieces_b = scatter(combined(distant_blocks))
    mine_a = spread(amp_a)
    other_a = swap(mine_a, "c")
    sums = [gamma(side, near_blocks, mine_a, other_a, None) for side in range(2)]
    amp_b = amplitudes(distant, pieces_b, CHIPS)
    mine_b = spread(amp_b)
    other_b = swap(after(mine_b, sums), "c")
    outs = []
    for side in range(2):
        here, there = gamma(side, distant_blocks, mine_b, other_b, sums[side])
        outs.append(here + swap(there, "yh").astype(F32))
    gamma_own, gamma_partner = outs
    return gamma_own, gamma_partner[None]


def solution(mesh):
    grid = Mesh(mesh.devices.reshape(SIZES), AXES)
    aux, virt = ("x", "yl", "c"), ("z", "yh")
    in_specs = (P(aux, virt), P(None, aux, virt), P(), P())
    out_specs = (P(aux, virt), P(None, aux, virt))
    return jax.shard_map(local, mesh=grid, in_specs=in_specs, out_specs=out_specs, check_vma=False)
```

```python
import functools

import jax
import jax.numpy as jnp
from jax import lax
from jax.experimental import pallas as pl
from jax.experimental.pallas import tpu as pltpu
from jax.sharding import Mesh, PartitionSpec as P

AXES = ("x", "yl", "c", "z", "yh")
SIZES = (4, 2, 2, 8, 2)
NZ = 8
CHIPS = 8
F32, BF16 = jnp.float32, jnp.bfloat16


def shift(value, axis, size, step):
    return lax.ppermute(value, axis, [(i, (i + step) % size) for i in range(size)])


def swap(value, axis):
    return lax.ppermute(value, axis, [(0, 1), (1, 0)])


class Lazy:
    def __init__(self, scratch, copy):
        self.scratch, self.copy = scratch, copy

    def get(self):
        if self.copy is not None:
            self.copy.wait()
            self.copy = None
        return self.scratch


def call(kernel, out_shape, *args, scalar=False, cost=0):
    lead = 1 if scalar else 0
    moved = args[lead:]
    count = len(moved)
    outs = len(jax.tree.leaves(out_shape))

    def body(*refs):
        sources = refs[lead:lead + count]
        targets = refs[lead + count:lead + count + outs]
        scratch = refs[lead + count + outs:-1]
        sems = refs[-1]
        lazy = []
        for index in range(count):
            copy = pltpu.make_async_copy(sources[index], scratch[index], sems.at[index])
            copy.start()
            lazy.append(Lazy(scratch[index], copy))
        kernel(*refs[:lead], *lazy, *targets)
        for item in lazy:
            item.get()

    specs = [pl.BlockSpec(memory_space=pltpu.SMEM)] * lead + [pl.BlockSpec(memory_space=pltpu.HBM)] * count
    out_specs = jax.tree.map(lambda _: pl.BlockSpec(memory_space=pltpu.VMEM), out_shape)
    return pl.pallas_call(
        body,
        out_shape=out_shape,
        in_specs=specs,
        out_specs=out_specs,
        scratch_shapes=[pltpu.VMEM(arg.shape, arg.dtype) for arg in moved] + [pltpu.SemaphoreType.DMA((count,))],
        cost_estimate=pl.CostEstimate(flops=cost, bytes_accessed=0, transcendentals=0),
        compiler_params=pltpu.CompilerParams(vmem_limit_bytes=56 * 1024 * 1024),
    )(*args)


def prepare_kernel(width, core, *refs):
    out = refs[-1]
    parts = [ref.get() for ref in refs[:-1]]
    count = len(parts) // 2
    zero = core[0] == 0
    start = 0
    for index in range(count):
        here, peer = parts[index], parts[count + index]
        rows = here.shape[0]
        for side in range(2):
            columns = slice(side * width, (side + 1) * width)
            first, second = here[:, columns].T, peer[:, columns].T
            into = slice(start, start + rows)
            out[2 * side * width:(2 * side + 1) * width, into] = jnp.where(zero, first, second)
            out[(2 * side + 1) * width:(2 * side + 2) * width, into] = jnp.where(zero, second, first)
        start += rows


def products_kernel(counts, width, *refs):
    left = refs[0].get()
    kept, given = refs[-1 - len(counts)], refs[-len(counts):]
    position = 1
    for index, count in enumerate(counts):
        parts = [ref.get() for ref in refs[position:position + count]]
        position += count
        for side in range(2):
            columns = slice(width, 2 * width) if side == 0 else slice(0, width)
            total = None
            start = 0
            for part in parts:
                rows = part.shape[0]
                value = jnp.dot(
                    left[2 * side * width:(2 * side + 2) * width, start:start + rows],
                    part[:, columns],
                    preferred_element_type=F32,
                )
                total = value if total is None else total + value
                start += rows
            place = slice((2 * index + side) * width, (2 * index + side + 1) * width)
            kept[:, place] = total[:width]
            given[index][:, side * width:(side + 1) * width] = total[width:]


def products(left, blocks, width, cost):
    counts = [len(block) for block in blocks]
    flat = [part for block in blocks for part in block]
    kept = jax.ShapeDtypeStruct((width, 2 * width * len(blocks)), F32)
    given = [jax.ShapeDtypeStruct((width, 2 * width), F32)] * len(blocks)
    kept, *given = call(functools.partial(products_kernel, counts, width), [kept, *given], left, *flat, cost=cost)
    return kept, given


def sum_kernel(counts, width, *refs):
    out = refs[-1]
    position = 0
    place = 0
    for count in counts:
        kept = refs[position].get()
        for index in range(count):
            columns = slice(index * 2 * width, (index + 1) * 2 * width)
            arrived = refs[position + 1 + index].get()
            out[:, place:place + 2 * width] = (kept[:, columns] + arrived[...]).astype(BF16)
            place += 2 * width
        position += count + 1


def amplitude_kernel(count, width, copies, pieces, row_level, col_energy, out):
    pieces, row_level, col_energy = pieces.get(), row_level.get(), col_energy.get()
    for index in range(count):
        denom = row_level[...] - col_energy[:, index * width:(index + 1) * width]
        direct = None
        crossed = None
        for chip in range(CHIPS):
            first = pieces[chip, :, (2 * index) * width:(2 * index + 1) * width].astype(F32)
            second = pieces[chip, :, (2 * index + 1) * width:(2 * index + 2) * width].astype(F32)
            direct = first if direct is None else direct + first
            crossed = second if crossed is None else crossed + second
        amp = ((2.0 * direct - crossed) / denom).astype(BF16)
        amp_crossed = ((2.0 * crossed - direct) / denom).astype(BF16)
        for copy in range(copies):
            out[copy, :, (2 * index) * width:(2 * index + 1) * width] = amp
            out[copy, :, (2 * index + 1) * width:(2 * index + 2) * width] = amp_crossed


def contract(block, amps):
    return lax.dot_general(block, amps, (((1,), (1,)), ((), ())), preferred_element_type=F32)


def gamma_kernel(counts, width, step, side, add, *refs):
    core, mine, other = refs[0], refs[1].get(), refs[2].get()
    count = len(counts)
    blocks = []
    position = 3
    for parts in counts:
        blocks.append([ref.get() for ref in refs[position:position + parts]])
        position += parts
    outs = refs[-2:]
    sums = [ref.get() for ref in refs[position:position + 2]] if add else None
    zero = core[0] == 0
    columns = slice(width, 2 * width) if side == 0 else slice(0, width)
    for store in range(2):
        chosen = zero if store == 0 else jnp.logical_not(zero)
        amps = []
        for index in range(count):
            place = slice((2 * index + side) * width, (2 * index + side + 1) * width)
            amps.append(jnp.where(chosen, mine[:, place], other[:, place]))
        for start in range(0, outs[store].shape[0], step):
            into = slice(start, start + step)
            total = None
            for index, parts in enumerate(blocks):
                size = parts[0].shape[0]
                rows = slice(start % size, start % size + step)
                value = contract(parts[start // size][rows, columns], amps[index])
                total = value if total is None else total + value
            if add:
                total = total + sums[store][into, :]
            outs[store][into, :] = total.astype(outs[store].dtype)


def local(own, partner_blocks, occ_energy, virt_energy):
    x, yl, c, z, yh = (lax.axis_index(name) for name in AXES)
    k = x * 2 + yl
    depth, width = own.shape
    half = depth // 2
    rows = width // CHIPS
    step = half
    first = c == 0
    core = c.astype(jnp.int32).reshape(1)

    base = jnp.concatenate([own, partner_blocks[0]], axis=1)
    base = (base,)
    base_peer = (swap(base[0], "yh"),)
    shape = jax.ShapeDtypeStruct((4 * width, depth), BF16)
    left = call(functools.partial(prepare_kernel, width), shape, core, *base, *base_peer, scalar=True)
    level = occ_energy[0] + occ_energy[1]
    row_energy = lax.dynamic_slice_in_dim(virt_energy, (z * 2 + (yh ^ c)) * width + k * rows, rows)
    row_level = (level - row_energy)[:, None]
    by_block = virt_energy.reshape(NZ, 2, width)
    col_energy = {d: lax.dynamic_slice(by_block, ((z + d) % NZ, yh, 0), (1, 1, width)).reshape(1, width) for d in range(-3, 5)}

    def after(values, *others):
        return lax.optimization_barrier((values, others))[0]

    def halves(blocks, cost=0):
        kept, given = products(left, blocks, width, cost)
        return kept, [swap(part, "c") for part in given]

    def scatter(sets):
        counts = [len(given) for _, given in sets]
        shape = jax.ShapeDtypeStruct((width, 2 * width * sum(counts)), BF16)
        flat = [part for kept, given in sets for part in [kept, *given]]
        summed = call(functools.partial(sum_kernel, counts, width), shape, *flat)
        return lax.all_to_all(summed.reshape(CHIPS, rows, -1), ("x", "yl"), 0, 0, tiled=True)

    def amplitudes(group, pieces, copies):
        cols = jnp.concatenate([col_energy[d] for d in group], axis=1)
        shape = jax.ShapeDtypeStruct((copies, rows, 2 * width * len(group)), BF16)
        kernel = functools.partial(amplitude_kernel, len(group), width, copies)
        return call(kernel, shape, pieces, row_level, cols)

    def spread(copies):
        return lax.all_to_all(copies, ("x", "yl"), 0, 0, tiled=True).reshape(width, -1)

    def gamma(side, blocks, mine, other, sums):
        kernel = functools.partial(gamma_kernel, [len(block) for block in blocks], width, step, side, sums is not None)
        shape = (depth, width)
        shapes = jax.ShapeDtypeStruct(shape, F32), jax.ShapeDtypeStruct(shape, F32 if sums is None else BF16)
        flat = [part for block in blocks for part in block]
        return call(kernel, shapes, core, mine, other, *flat, *(sums or ()), scalar=True)

    def both(parts, way):
        return tuple(shift(part, "z", NZ, way) for part in parts)

    up1, down1 = both(base, 1), both(base, -1)
    up2, down2 = both(up1, 1), both(down1, -1)
    up3, down3 = both(up2, 1), both(down2, -1)
    far = shift(up3[0][:half], "z", NZ, 1), shift(down3[0][half:], "z", NZ, -1)
    near, distant = (0, 1, -1), (2, -2, 3, -3, 4)
    near_blocks, distant_blocks = [base, down1, up1], [down2, up2, down3, up3, far]
    pieces_a = scatter([after(halves(near_blocks), up2, down2)])
    amp_a = amplitudes(near, after(pieces_a, up3, down3), CHIPS)
    mine_a = spread(amp_a)
    other_a = swap(mine_a, "c")
    middle_halves = halves(after(distant_blocks[:2], pieces_a))
    last_halves = halves(distant_blocks[2:])
    pieces_b = scatter([after(middle_halves, far), after(last_halves, mine_a)])
    sums = [gamma(side, near_blocks, mine_a, other_a, None) for side in range(2)]
    amp_b = amplitudes(distant, after(pieces_b, sums), CHIPS)
    mine_b = spread(amp_b)
    other_b = swap(mine_b, "c")
    outs = []
    for side in range(2):
        here, there = gamma(side, distant_blocks, mine_b, other_b, sums[side])
        outs.append(here + swap(there, "yh").astype(F32))
    gamma_own, gamma_partner = outs
    return gamma_own, gamma_partner[None]


def solution(mesh):
    grid = Mesh(mesh.devices.reshape(SIZES), AXES)
    aux, virt = ("x", "yl", "c"), ("z", "yh")
    in_specs = (P(aux, virt), P(None, aux, virt), P(), P())
    out_specs = (P(aux, virt), P(None, aux, virt))
    return jax.shard_map(local, mesh=grid, in_specs=in_specs, out_specs=out_specs, check_vma=False)
```

```python
import functools

import jax
import jax.numpy as jnp
from jax import lax
from jax.experimental import pallas as pl
from jax.experimental.pallas import tpu as pltpu
from jax.sharding import Mesh, PartitionSpec as P

AXES = ("x", "yl", "c", "z", "yh")
SIZES = (4, 2, 2, 8, 2)
NZ = 8
CHIPS = 8
F32, BF16 = jnp.float32, jnp.bfloat16


def shift(value, axis, size, step):
    return lax.ppermute(value, axis, [(i, (i + step) % size) for i in range(size)])


def swap(value, axis):
    return lax.ppermute(value, axis, [(0, 1), (1, 0)])


class Lazy:
    def __init__(self, scratch, copy):
        self.scratch, self.copy = scratch, copy

    def get(self):
        if self.copy is not None:
            self.copy.wait()
            self.copy = None
        return self.scratch


def call(kernel, out_shape, *args, scalar=False, cost=0):
    lead = 1 if scalar else 0
    moved = args[lead:]
    count = len(moved)
    outs = len(jax.tree.leaves(out_shape))

    def body(*refs):
        sources = refs[lead:lead + count]
        targets = refs[lead + count:lead + count + outs]
        scratch = refs[lead + count + outs:-1]
        sems = refs[-1]
        lazy = []
        for index in range(count):
            copy = pltpu.make_async_copy(sources[index], scratch[index], sems.at[index])
            copy.start()
            lazy.append(Lazy(scratch[index], copy))
        kernel(*refs[:lead], *lazy, *targets)
        for item in lazy:
            item.get()

    specs = [pl.BlockSpec(memory_space=pltpu.SMEM)] * lead + [pl.BlockSpec(memory_space=pltpu.HBM)] * count
    out_specs = jax.tree.map(lambda _: pl.BlockSpec(memory_space=pltpu.VMEM), out_shape)
    return pl.pallas_call(
        body,
        out_shape=out_shape,
        in_specs=specs,
        out_specs=out_specs,
        scratch_shapes=[pltpu.VMEM(arg.shape, arg.dtype) for arg in moved] + [pltpu.SemaphoreType.DMA((count,))],
        cost_estimate=pl.CostEstimate(flops=cost, bytes_accessed=0, transcendentals=0),
        compiler_params=pltpu.CompilerParams(vmem_limit_bytes=56 * 1024 * 1024),
    )(*args)


def prepare_kernel(width, core, *refs):
    out = refs[-1]
    parts = [ref.get() for ref in refs[:-1]]
    count = len(parts) // 2
    zero = core[0] == 0
    start = 0
    for index in range(count):
        here, peer = parts[index], parts[count + index]
        rows = here.shape[0]
        for side in range(2):
            columns = slice(side * width, (side + 1) * width)
            first, second = here[:, columns].T, peer[:, columns].T
            into = slice(start, start + rows)
            out[2 * side * width:(2 * side + 1) * width, into] = jnp.where(zero, first, second)
            out[(2 * side + 1) * width:(2 * side + 2) * width, into] = jnp.where(zero, second, first)
        start += rows


def products_kernel(counts, width, *refs):
    left = refs[0].get()
    kept, given = refs[-1 - len(counts)], refs[-len(counts):]
    position = 1
    for index, count in enumerate(counts):
        parts = [ref.get() for ref in refs[position:position + count]]
        position += count
        for side in range(2):
            columns = slice(width, 2 * width) if side == 0 else slice(0, width)
            total = None
            start = 0
            for part in parts:
                rows = part.shape[0]
                value = jnp.dot(
                    left[2 * side * width:(2 * side + 2) * width, start:start + rows],
                    part[:, columns],
                    preferred_element_type=F32,
                )
                total = value if total is None else total + value
                start += rows
            place = slice((2 * index + side) * width, (2 * index + side + 1) * width)
            kept[:, place] = total[:width]
            given[index][:, side * width:(side + 1) * width] = total[width:]


def products(left, blocks, width, cost):
    counts = [len(block) for block in blocks]
    flat = [part for block in blocks for part in block]
    kept = jax.ShapeDtypeStruct((width, 2 * width * len(blocks)), F32)
    given = [jax.ShapeDtypeStruct((width, 2 * width), F32)] * len(blocks)
    kept, *given = call(functools.partial(products_kernel, counts, width), [kept, *given], left, *flat, cost=cost)
    return kept, given


def sum_kernel(counts, width, *refs):
    out = refs[-1]
    position = 0
    place = 0
    for count in counts:
        kept = refs[position].get()
        for index in range(count):
            columns = slice(index * 2 * width, (index + 1) * 2 * width)
            arrived = refs[position + 1 + index].get()
            out[:, place:place + 2 * width] = (kept[:, columns] + arrived[...]).astype(BF16)
            place += 2 * width
        position += count + 1


def amplitude_kernel(count, width, copies, pieces, row_level, col_energy, out):
    pieces, row_level, col_energy = pieces.get(), row_level.get(), col_energy.get()
    for index in range(count):
        denom = row_level[...] - col_energy[:, index * width:(index + 1) * width]
        direct = None
        crossed = None
        for chip in range(CHIPS):
            first = pieces[chip, :, (2 * index) * width:(2 * index + 1) * width].astype(F32)
            second = pieces[chip, :, (2 * index + 1) * width:(2 * index + 2) * width].astype(F32)
            direct = first if direct is None else direct + first
            crossed = second if crossed is None else crossed + second
        amp = ((2.0 * direct - crossed) / denom).astype(BF16)
        amp_crossed = ((2.0 * crossed - direct) / denom).astype(BF16)
        for copy in range(copies):
            out[copy, :, (2 * index) * width:(2 * index + 1) * width] = amp
            out[copy, :, (2 * index + 1) * width:(2 * index + 2) * width] = amp_crossed


def contract(block, amps):
    return lax.dot_general(block, amps, (((1,), (1,)), ((), ())), preferred_element_type=F32)


def gamma_kernel(counts, width, step, side, store, add, *refs):
    core, mine, other = refs[0], refs[1].get(), refs[2].get()
    count = len(counts)
    blocks = []
    position = 3
    for parts in counts:
        blocks.append([ref.get() for ref in refs[position:position + parts]])
        position += parts
    out = refs[-1]
    before = refs[position].get() if add else None
    zero = core[0] == 0
    columns = slice(width, 2 * width) if side == 0 else slice(0, width)
    chosen = zero if store == 0 else jnp.logical_not(zero)
    amps = []
    for index in range(count):
        place = slice((2 * index + side) * width, (2 * index + side + 1) * width)
        amps.append(jnp.where(chosen, mine[:, place], other[:, place]))
    for start in range(0, out.shape[0], step):
        into = slice(start, start + step)
        total = None
        for index, parts in enumerate(blocks):
            size = parts[0].shape[0]
            rows = slice(start % size, start % size + step)
            value = contract(parts[start // size][rows, columns], amps[index])
            total = value if total is None else total + value
        if add:
            total = total + before[into, :]
        out[into, :] = total.astype(out.dtype)


def local(own, partner_blocks, occ_energy, virt_energy):
    x, yl, c, z, yh = (lax.axis_index(name) for name in AXES)
    k = x * 2 + yl
    depth, width = own.shape
    half = depth // 2
    rows = width // CHIPS
    step = half
    first = c == 0
    core = c.astype(jnp.int32).reshape(1)

    base = jnp.concatenate([own, partner_blocks[0]], axis=1)
    base = (base,)
    base_peer = (swap(base[0], "yh"),)
    shape = jax.ShapeDtypeStruct((4 * width, depth), BF16)
    left = call(functools.partial(prepare_kernel, width), shape, core, *base, *base_peer, scalar=True)
    level = occ_energy[0] + occ_energy[1]
    row_energy = lax.dynamic_slice_in_dim(virt_energy, (z * 2 + (yh ^ c)) * width + k * rows, rows)
    row_level = (level - row_energy)[:, None]
    by_block = virt_energy.reshape(NZ, 2, width)
    col_energy = {d: lax.dynamic_slice(by_block, ((z + d) % NZ, yh, 0), (1, 1, width)).reshape(1, width) for d in range(-3, 5)}

    def after(values, *others):
        return lax.optimization_barrier((values, others))[0]

    def halves(blocks, cost=0):
        kept, given = products(left, blocks, width, cost)
        return kept, [swap(part, "c") for part in given]

    def scatter(sets):
        counts = [len(given) for _, given in sets]
        shape = jax.ShapeDtypeStruct((width, 2 * width * sum(counts)), BF16)
        flat = [part for kept, given in sets for part in [kept, *given]]
        summed = call(functools.partial(sum_kernel, counts, width), shape, *flat)
        return lax.all_to_all(summed.reshape(CHIPS, rows, -1), ("x", "yl"), 0, 0, tiled=True)

    def amplitudes(group, pieces, copies):
        cols = jnp.concatenate([col_energy[d] for d in group], axis=1)
        shape = jax.ShapeDtypeStruct((copies, rows, 2 * width * len(group)), BF16)
        kernel = functools.partial(amplitude_kernel, len(group), width, copies)
        return call(kernel, shape, pieces, row_level, cols)

    def spread(copies):
        return lax.all_to_all(copies, ("x", "yl"), 0, 0, tiled=True).reshape(width, -1)

    def gamma(side, store, blocks, mine, other, before=None, dtype=F32):
        counts = [len(block) for block in blocks]
        kernel = functools.partial(gamma_kernel, counts, width, step, side, store, before is not None)
        flat = [part for block in blocks for part in block]
        extra = [] if before is None else [before]
        return call(kernel, jax.ShapeDtypeStruct((depth, width), dtype), core, mine, other, *flat, *extra, scalar=True)

    def both(parts, way):
        return tuple(shift(part, "z", NZ, way) for part in parts)

    up1, down1 = both(base, 1), both(base, -1)
    up1, down1 = after((up1, down1), base_peer)
    up2, down2 = both(up1, 1), both(down1, -1)
    near, distant = (0, 1, -1), (2, -2, 3, -3, 4)
    near_blocks = [base, down1, up1]
    near_halves = halves(near_blocks)
    (up2, down2), near_halves = lax.optimization_barrier(((up2, down2), near_halves))
    up3, down3 = both(up2, 1), both(down2, -1)
    far = shift(up3[0][:half], "z", NZ, 1), shift(down3[0][half:], "z", NZ, -1)

    distant_blocks = [down2, up2, down3, up3, far]
    pieces_a = scatter([near_halves])
    amp_a = amplitudes(near, after(pieces_a, up3, down3), CHIPS)
    mine_a = spread(amp_a)
    other_a = swap(mine_a, "c")
    middle_halves = halves(after(distant_blocks[:2], pieces_a))
    last_halves = halves(distant_blocks[2:])
    pieces_b = scatter([after(middle_halves, far), after(last_halves, mine_a)])
    sums = [[gamma(side, store, near_blocks, mine_a, other_a) for store in range(2)] for side in range(2)]
    amp_b = amplitudes(distant, after(pieces_b, sums), CHIPS)
    mine_b = spread(amp_b)
    other_b = swap(mine_b, "c")
    there = [gamma(side, 1, distant_blocks, mine_b, other_b, sums[side][1], BF16) for side in range(2)]
    arrived = [swap(part, "yh").astype(F32) for part in there]
    mine_b, other_b = after((mine_b, other_b), there)
    here = [gamma(side, 0, distant_blocks, mine_b, other_b, sums[side][0]) for side in range(2)]
    gamma_own, gamma_partner = (here[side] + arrived[side] for side in range(2))
    return gamma_own, gamma_partner[None]


def solution(mesh):
    grid = Mesh(mesh.devices.reshape(SIZES), AXES)
    aux, virt = ("x", "yl", "c"), ("z", "yh")
    in_specs = (P(aux, virt), P(None, aux, virt), P(), P())
    out_specs = (P(aux, virt), P(None, aux, virt))
    return jax.shard_map(local, mesh=grid, in_specs=in_specs, out_specs=out_specs, check_vma=False)
```

```python
import functools

import jax
import jax.numpy as jnp
from jax import lax
from jax.experimental import pallas as pl
from jax.experimental.pallas import tpu as pltpu
from jax.sharding import Mesh, PartitionSpec as P

AXES = ("x", "yl", "c", "z", "yh")
SIZES = (4, 2, 2, 8, 2)
NZ = 8
CHIPS = 8
F32, BF16 = jnp.float32, jnp.bfloat16


def shift(value, axis, size, step):
    return lax.ppermute(value, axis, [(i, (i + step) % size) for i in range(size)])


def swap(value, axis):
    return lax.ppermute(value, axis, [(0, 1), (1, 0)])


class Lazy:
    def __init__(self, scratch, copy):
        self.scratch, self.copy = scratch, copy

    def get(self):
        if self.copy is not None:
            self.copy.wait()
            self.copy = None
        return self.scratch


def call(kernel, out_shape, *args, scalar=False, cost=0):
    lead = 1 if scalar else 0
    windows = [arg[1] if isinstance(arg, tuple) else None for arg in args[lead:]]
    args = [arg[0] if isinstance(arg, tuple) else arg for arg in args]
    moved = args[lead:]
    count = len(moved)
    outs = len(jax.tree.leaves(out_shape))

    def body(*refs):
        sources = refs[lead:lead + count]
        targets = refs[lead + count:lead + count + outs]
        scratch = refs[lead + count + outs:-1]
        sems = refs[-1]
        lazy = []
        for index in range(count):
            source = sources[index]
            if windows[index] is not None:
                source = source.at[:, windows[index]]
            copy = pltpu.make_async_copy(source, scratch[index], sems.at[index])
            copy.start()
            lazy.append(Lazy(scratch[index], copy))
        kernel(*refs[:lead], *lazy, *targets)
        for item in lazy:
            item.get()

    buffers = []
    for arg, window in zip(moved, windows):
        shape = arg.shape if window is None else (arg.shape[0], window.stop - window.start)
        buffers.append(pltpu.VMEM(shape, arg.dtype))
    specs = [pl.BlockSpec(memory_space=pltpu.SMEM)] * lead + [pl.BlockSpec(memory_space=pltpu.HBM)] * count
    out_specs = jax.tree.map(lambda _: pl.BlockSpec(memory_space=pltpu.VMEM), out_shape)
    return pl.pallas_call(
        body,
        out_shape=out_shape,
        in_specs=specs,
        out_specs=out_specs,
        scratch_shapes=buffers + [pltpu.SemaphoreType.DMA((count,))],
        cost_estimate=pl.CostEstimate(flops=cost, bytes_accessed=0, transcendentals=0),
        compiler_params=pltpu.CompilerParams(vmem_limit_bytes=56 * 1024 * 1024),
    )(*args)


def prepare_kernel(width, core, *refs):
    out = refs[-1]
    parts = [ref.get() for ref in refs[:-1]]
    count = len(parts) // 2
    zero = core[0] == 0
    start = 0
    for index in range(count):
        here, peer = parts[index], parts[count + index]
        rows = here.shape[0]
        for side in range(2):
            columns = slice(side * width, (side + 1) * width)
            first, second = here[:, columns].T, peer[:, columns].T
            into = slice(start, start + rows)
            out[2 * side * width:(2 * side + 1) * width, into] = jnp.where(zero, first, second)
            out[(2 * side + 1) * width:(2 * side + 2) * width, into] = jnp.where(zero, second, first)
        start += rows


def products_kernel(counts, width, *refs):
    left = refs[0].get()
    kept, given = refs[-1 - len(counts)], refs[-len(counts):]
    position = 1
    for index, count in enumerate(counts):
        parts = [ref.get() for ref in refs[position:position + count]]
        position += count
        for side in range(2):
            columns = slice(width, 2 * width) if side == 0 else slice(0, width)
            total = None
            start = 0
            for part in parts:
                rows = part.shape[0]
                value = jnp.dot(
                    left[2 * side * width:(2 * side + 2) * width, start:start + rows],
                    part[:, columns],
                    preferred_element_type=F32,
                )
                total = value if total is None else total + value
                start += rows
            place = slice((2 * index + side) * width, (2 * index + side + 1) * width)
            kept[:, place] = total[:width]
            given[index][:, side * width:(side + 1) * width] = total[width:]


def products(left, blocks, width, cost):
    counts = [len(block) for block in blocks]
    flat = [part for block in blocks for part in block]
    kept = jax.ShapeDtypeStruct((width, 2 * width * len(blocks)), F32)
    given = [jax.ShapeDtypeStruct((width, 2 * width), F32)] * len(blocks)
    kept, *given = call(functools.partial(products_kernel, counts, width), [kept, *given], left, *flat, cost=cost)
    return kept, given


def sum_kernel(counts, width, *refs):
    out = refs[-1]
    position = 0
    place = 0
    for count in counts:
        kept = refs[position].get()
        for index in range(count):
            columns = slice(index * 2 * width, (index + 1) * 2 * width)
            arrived = refs[position + 1 + index].get()
            out[:, place:place + 2 * width] = (kept[:, columns] + arrived[...]).astype(BF16)
            place += 2 * width
        position += count + 1


def amplitude_kernel(count, width, copies, pieces, row_level, col_energy, out):
    pieces, row_level, col_energy = pieces.get(), row_level.get(), col_energy.get()
    for index in range(count):
        denom = row_level[...] - col_energy[:, index * width:(index + 1) * width]
        direct = None
        crossed = None
        for chip in range(CHIPS):
            first = pieces[chip, :, (2 * index) * width:(2 * index + 1) * width].astype(F32)
            second = pieces[chip, :, (2 * index + 1) * width:(2 * index + 2) * width].astype(F32)
            direct = first if direct is None else direct + first
            crossed = second if crossed is None else crossed + second
        amp = ((2.0 * direct - crossed) / denom).astype(BF16)
        amp_crossed = ((2.0 * crossed - direct) / denom).astype(BF16)
        for copy in range(copies):
            out[copy, :, (2 * index) * width:(2 * index + 1) * width] = amp
            out[copy, :, (2 * index + 1) * width:(2 * index + 2) * width] = amp_crossed


def contract(block, amps):
    return lax.dot_general(block, amps, (((1,), (1,)), ((), ())), preferred_element_type=F32)


def gamma_kernel(counts, width, step, side, store, add, *refs):
    core, mine, other = refs[0], refs[1].get(), refs[2].get()
    count = len(counts)
    blocks = []
    position = 3
    for parts in counts:
        blocks.append([ref.get() for ref in refs[position:position + parts]])
        position += parts
    out = refs[-1]
    before = refs[position].get() if add else None
    zero = core[0] == 0
    chosen = zero if store == 0 else jnp.logical_not(zero)
    amps = []
    for index in range(count):
        place = slice((2 * index + side) * width, (2 * index + side + 1) * width)
        amps.append(jnp.where(chosen, mine[:, place], other[:, place]))
    for start in range(0, out.shape[0], step):
        into = slice(start, start + step)
        total = None
        for index, parts in enumerate(blocks):
            size = parts[0].shape[0]
            rows = slice(start % size, start % size + step)
            value = contract(parts[start // size][rows, :], amps[index])
            total = value if total is None else total + value
        if add:
            total = total + before[into, :]
        out[into, :] = total.astype(out.dtype)


def local(own, partner_blocks, occ_energy, virt_energy):
    x, yl, c, z, yh = (lax.axis_index(name) for name in AXES)
    k = x * 2 + yl
    depth, width = own.shape
    half = depth // 2
    rows = width // CHIPS
    step = half
    first = c == 0
    core = c.astype(jnp.int32).reshape(1)

    base = jnp.concatenate([own, partner_blocks[0]], axis=1)
    base = (base,)
    base_peer = (swap(base[0], "yh"),)
    shape = jax.ShapeDtypeStruct((4 * width, depth), BF16)
    left = call(functools.partial(prepare_kernel, width), shape, core, *base, *base_peer, scalar=True)
    level = occ_energy[0] + occ_energy[1]
    row_energy = lax.dynamic_slice_in_dim(virt_energy, (z * 2 + (yh ^ c)) * width + k * rows, rows)
    row_level = (level - row_energy)[:, None]
    by_block = virt_energy.reshape(NZ, 2, width)
    col_energy = {d: lax.dynamic_slice(by_block, ((z + d) % NZ, yh, 0), (1, 1, width)).reshape(1, width) for d in range(-3, 5)}

    def after(values, *others):
        return lax.optimization_barrier((values, others))[0]

    def halves(blocks, cost=0):
        kept, given = products(left, blocks, width, cost)
        return kept, [swap(part, "c") for part in given]

    def scatter(sets):
        counts = [len(given) for _, given in sets]
        shape = jax.ShapeDtypeStruct((width, 2 * width * sum(counts)), BF16)
        flat = [part for kept, given in sets for part in [kept, *given]]
        summed = call(functools.partial(sum_kernel, counts, width), shape, *flat)
        return lax.all_to_all(summed.reshape(CHIPS, rows, -1), ("x", "yl"), 0, 0, tiled=True)

    def amplitudes(group, pieces, copies):
        cols = jnp.concatenate([col_energy[d] for d in group], axis=1)
        shape = jax.ShapeDtypeStruct((copies, rows, 2 * width * len(group)), BF16)
        kernel = functools.partial(amplitude_kernel, len(group), width, copies)
        return call(kernel, shape, pieces, row_level, cols)

    def spread(copies):
        return lax.all_to_all(copies, ("x", "yl"), 0, 0, tiled=True).reshape(width, -1)

    def gamma(side, store, blocks, mine, other, before=None, dtype=F32):
        counts = [len(block) for block in blocks]
        kernel = functools.partial(gamma_kernel, counts, width, step, side, store, before is not None)
        columns = slice(width, 2 * width) if side == 0 else slice(0, width)
        flat = [(part, columns) for block in blocks for part in block]
        extra = [] if before is None else [before]
        return call(kernel, jax.ShapeDtypeStruct((depth, width), dtype), core, mine, other, *flat, *extra, scalar=True)

    def both(parts, way):
        return tuple(shift(part, "z", NZ, way) for part in parts)

    up1, down1 = both(base, 1), both(base, -1)
    up1, down1 = after((up1, down1), base_peer)
    up2, down2 = both(up1, 1), both(down1, -1)
    near, distant = (0, 1, -1), (2, -2, 3, -3, 4)
    near_blocks = [base, down1, up1]
    near_halves = halves(near_blocks)
    (up2, down2), near_halves = lax.optimization_barrier(((up2, down2), near_halves))
    up3, down3 = both(up2, 1), both(down2, -1)
    pieces_a = scatter([near_halves])
    middle_halves = halves([down2, up2])
    (up3, down3), middle_halves = lax.optimization_barrier(((up3, down3), middle_halves))
    far = shift(up3[0][:half], "z", NZ, 1), shift(down3[0][half:], "z", NZ, -1)

    distant_blocks = [down2, up2, down3, up3, far]
    amp_a = amplitudes(near, pieces_a, CHIPS)
    mine_a = spread(amp_a)
    other_a = swap(mine_a, "c")
    third_halves = halves([down3, up3])
    last, third_halves = lax.optimization_barrier((far, third_halves))
    last_halves = halves([last])
    pieces_b = scatter([middle_halves, third_halves, after(last_halves, mine_a)])
    sums = [[gamma(side, store, near_blocks, mine_a, other_a) for store in range(2)] for side in range(2)]
    amp_b = amplitudes(distant, after(pieces_b, sums), CHIPS)
    mine_b = spread(amp_b)
    other_b = swap(mine_b, "c")
    there = [gamma(side, 1, distant_blocks, mine_b, other_b, sums[side][1], BF16) for side in range(2)]
    arrived = [swap(part, "yh").astype(F32) for part in there]
    mine_b, other_b = after((mine_b, other_b), there)
    here = [gamma(side, 0, distant_blocks, mine_b, other_b, sums[side][0]) for side in range(2)]
    gamma_own, gamma_partner = (here[side] + arrived[side] for side in range(2))
    return gamma_own, gamma_partner[None]


def solution(mesh):
    grid = Mesh(mesh.devices.reshape(SIZES), AXES)
    aux, virt = ("x", "yl", "c"), ("z", "yh")
    in_specs = (P(aux, virt), P(None, aux, virt), P(), P())
    out_specs = (P(aux, virt), P(None, aux, virt))
    return jax.shard_map(local, mesh=grid, in_specs=in_specs, out_specs=out_specs, check_vma=False)
```

```python
import functools

import jax
import jax.numpy as jnp
from jax import lax
from jax.experimental import pallas as pl
from jax.experimental.pallas import tpu as pltpu
from jax.sharding import Mesh, PartitionSpec as P

AXES = ("x", "yl", "c", "z", "yh")
SIZES = (4, 2, 2, 8, 2)
NZ = 8
CHIPS = 8
F32, BF16 = jnp.float32, jnp.bfloat16


def shift(value, axis, size, step):
    return lax.ppermute(value, axis, [(i, (i + step) % size) for i in range(size)])


def swap(value, axis):
    return lax.ppermute(value, axis, [(0, 1), (1, 0)])


class Lazy:
    def __init__(self, scratch, copy):
        self.scratch, self.copy = scratch, copy

    def get(self):
        if self.copy is not None:
            self.copy.wait()
            self.copy = None
        return self.scratch


def call(kernel, out_shape, *args, scalar=False, cost=0):
    lead = 1 if scalar else 0
    windows = [arg[1] if isinstance(arg, tuple) else None for arg in args[lead:]]
    args = [arg[0] if isinstance(arg, tuple) else arg for arg in args]
    moved = args[lead:]
    count = len(moved)
    outs = len(jax.tree.leaves(out_shape))

    def body(*refs):
        sources = refs[lead:lead + count]
        targets = refs[lead + count:lead + count + outs]
        scratch = refs[lead + count + outs:-1]
        sems = refs[-1]
        lazy = []
        for index in range(count):
            source = sources[index]
            if windows[index] is not None:
                source = source.at[:, windows[index]]
            copy = pltpu.make_async_copy(source, scratch[index], sems.at[index])
            copy.start()
            lazy.append(Lazy(scratch[index], copy))
        kernel(*refs[:lead], *lazy, *targets)
        for item in lazy:
            item.get()

    buffers = []
    for arg, window in zip(moved, windows):
        shape = arg.shape if window is None else (arg.shape[0], window.stop - window.start)
        buffers.append(pltpu.VMEM(shape, arg.dtype))
    specs = [pl.BlockSpec(memory_space=pltpu.SMEM)] * lead + [pl.BlockSpec(memory_space=pltpu.HBM)] * count
    out_specs = jax.tree.map(lambda _: pl.BlockSpec(memory_space=pltpu.VMEM), out_shape)
    return pl.pallas_call(
        body,
        out_shape=out_shape,
        in_specs=specs,
        out_specs=out_specs,
        scratch_shapes=buffers + [pltpu.SemaphoreType.DMA((count,))],
        cost_estimate=pl.CostEstimate(flops=cost, bytes_accessed=0, transcendentals=0),
        compiler_params=pltpu.CompilerParams(vmem_limit_bytes=56 * 1024 * 1024),
    )(*args)


def prepare_kernel(width, core, *refs):
    out = refs[-1]
    parts = [ref.get() for ref in refs[:-1]]
    count = len(parts) // 2
    zero = core[0] == 0
    start = 0
    for index in range(count):
        here, peer = parts[index], parts[count + index]
        rows = here.shape[0]
        for side in range(2):
            columns = slice(side * width, (side + 1) * width)
            first, second = here[:, columns].T, peer[:, columns].T
            into = slice(start, start + rows)
            out[2 * side * width:(2 * side + 1) * width, into] = jnp.where(zero, first, second)
            out[(2 * side + 1) * width:(2 * side + 2) * width, into] = jnp.where(zero, second, first)
        start += rows


def products_kernel(counts, width, *refs):
    left = refs[0].get()
    kept, given = refs[-1 - len(counts)], refs[-len(counts):]
    position = 1
    for index, count in enumerate(counts):
        parts = [ref.get() for ref in refs[position:position + count]]
        position += count
        for side in range(2):
            columns = slice(width, 2 * width) if side == 0 else slice(0, width)
            total = None
            start = 0
            for part in parts:
                rows = part.shape[0]
                value = jnp.dot(
                    left[2 * side * width:(2 * side + 2) * width, start:start + rows],
                    part[:, columns],
                    preferred_element_type=F32,
                )
                total = value if total is None else total + value
                start += rows
            place = slice((2 * index + side) * width, (2 * index + side + 1) * width)
            kept[:, place] = total[:width]
            given[index][:, side * width:(side + 1) * width] = total[width:]


def products(left, blocks, width, cost):
    counts = [len(block) for block in blocks]
    flat = [part for block in blocks for part in block]
    kept = jax.ShapeDtypeStruct((width, 2 * width * len(blocks)), F32)
    given = [jax.ShapeDtypeStruct((width, 2 * width), F32)] * len(blocks)
    kept, *given = call(functools.partial(products_kernel, counts, width), [kept, *given], left, *flat, cost=cost)
    return kept, given


def sum_kernel(counts, width, *refs):
    out = refs[-1]
    position = 0
    place = 0
    for count in counts:
        kept = refs[position].get()
        for index in range(count):
            columns = slice(index * 2 * width, (index + 1) * 2 * width)
            arrived = refs[position + 1 + index].get()
            out[:, place:place + 2 * width] = (kept[:, columns] + arrived[...]).astype(BF16)
            place += 2 * width
        position += count + 1


def amplitude_kernel(count, width, copies, pieces, row_level, col_energy, out):
    pieces, row_level, col_energy = pieces.get(), row_level.get(), col_energy.get()
    for index in range(count):
        denom = row_level[...] - col_energy[:, index * width:(index + 1) * width]
        direct = None
        crossed = None
        for chip in range(CHIPS):
            first = pieces[chip, :, (2 * index) * width:(2 * index + 1) * width].astype(F32)
            second = pieces[chip, :, (2 * index + 1) * width:(2 * index + 2) * width].astype(F32)
            direct = first if direct is None else direct + first
            crossed = second if crossed is None else crossed + second
        amp = ((2.0 * direct - crossed) / denom).astype(BF16)
        amp_crossed = ((2.0 * crossed - direct) / denom).astype(BF16)
        for copy in range(copies):
            out[copy, :, (2 * index) * width:(2 * index + 1) * width] = amp
            out[copy, :, (2 * index + 1) * width:(2 * index + 2) * width] = amp_crossed


def contract(block, amps):
    return lax.dot_general(block, amps, (((1,), (1,)), ((), ())), preferred_element_type=F32)


def gamma_kernel(counts, width, step, side, store, add, *refs):
    core, mine, other = refs[0], refs[1].get(), refs[2].get()
    count = len(counts)
    blocks = []
    position = 3
    for parts in counts:
        blocks.append([ref.get() for ref in refs[position:position + parts]])
        position += parts
    out = refs[-1]
    before = refs[position].get() if add else None
    zero = core[0] == 0
    chosen = zero if store == 0 else jnp.logical_not(zero)
    amps = []
    for index in range(count):
        place = slice((2 * index + side) * width, (2 * index + side + 1) * width)
        amps.append(jnp.where(chosen, mine[:, place], other[:, place]))
    for start in range(0, out.shape[0], step):
        into = slice(start, start + step)
        total = None
        for index, parts in enumerate(blocks):
            size = parts[0].shape[0]
            rows = slice(start % size, start % size + step)
            value = contract(parts[start // size][rows, :], amps[index])
            total = value if total is None else total + value
        if add:
            total = total + before[into, :]
        out[into, :] = total.astype(out.dtype)


def local(own, partner_blocks, occ_energy, virt_energy):
    x, yl, c, z, yh = (lax.axis_index(name) for name in AXES)
    k = x * 2 + yl
    depth, width = own.shape
    half = depth // 2
    rows = width // CHIPS
    step = half
    first = c == 0
    core = c.astype(jnp.int32).reshape(1)

    base = jnp.concatenate([own, partner_blocks[0]], axis=1)
    base = (base,)
    base_peer = (swap(base[0], "yh"),)
    shape = jax.ShapeDtypeStruct((4 * width, depth), BF16)
    left = call(functools.partial(prepare_kernel, width), shape, core, *base, *base_peer, scalar=True)
    level = occ_energy[0] + occ_energy[1]
    row_energy = lax.dynamic_slice_in_dim(virt_energy, (z * 2 + (yh ^ c)) * width + k * rows, rows)
    row_level = (level - row_energy)[:, None]
    by_block = virt_energy.reshape(NZ, 2, width)
    col_energy = {d: lax.dynamic_slice(by_block, ((z + d) % NZ, yh, 0), (1, 1, width)).reshape(1, width) for d in range(-3, 5)}

    def after(values, *others):
        return lax.optimization_barrier((values, others))[0]

    def halves(blocks, cost=0):
        kept, given = products(left, blocks, width, cost)
        return kept, [swap(part, "c") for part in given]

    def added(sets):
        counts = [len(given) for _, given in sets]
        shape = jax.ShapeDtypeStruct((width, 2 * width * sum(counts)), BF16)
        flat = [part for kept, given in sets for part in [kept, *given]]
        return call(functools.partial(sum_kernel, counts, width), shape, *flat)

    def scatter(summed):
        return lax.all_to_all(summed.reshape(CHIPS, rows, -1), ("x", "yl"), 0, 0, tiled=True)

    def amplitudes(group, pieces, copies):
        cols = jnp.concatenate([col_energy[d] for d in group], axis=1)
        shape = jax.ShapeDtypeStruct((copies, rows, 2 * width * len(group)), BF16)
        kernel = functools.partial(amplitude_kernel, len(group), width, copies)
        return call(kernel, shape, pieces, row_level, cols)

    def spread(copies):
        return lax.all_to_all(copies, ("x", "yl"), 0, 0, tiled=True).reshape(width, -1)

    def gamma(side, store, blocks, mine, other, before=None, dtype=F32):
        counts = [len(block) for block in blocks]
        kernel = functools.partial(gamma_kernel, counts, width, step, side, store, before is not None)
        columns = slice(width, 2 * width) if side == 0 else slice(0, width)
        flat = [(part, columns) for block in blocks for part in block]
        extra = [] if before is None else [before]
        return call(kernel, jax.ShapeDtypeStruct((depth, width), dtype), core, mine, other, *flat, *extra, scalar=True)

    def both(parts, way):
        return tuple(shift(part, "z", NZ, way) for part in parts)

    up1, down1 = both(base, 1), both(base, -1)
    up1, down1 = after((up1, down1), base_peer)
    up2, down2 = both(up1, 1), both(down1, -1)
    near, distant = (0, 1, -1), (2, -2, 3, -3, 4)
    near_blocks = [base, down1, up1]
    near_halves = halves(near_blocks)
    (up2, down2), near_halves = lax.optimization_barrier(((up2, down2), near_halves))
    up3, down3 = both(up2, 1), both(down2, -1)
    summed_a = added([near_halves])
    pieces_a = scatter(summed_a)
    middle_halves = halves(after([down2, up2], summed_a))
    (up3, down3), middle_halves = lax.optimization_barrier(((up3, down3), middle_halves))
    far = shift(up3[0][:half], "z", NZ, 1), shift(down3[0][half:], "z", NZ, -1)

    distant_blocks = [down2, up2, down3, up3, far]
    amp_a = amplitudes(near, pieces_a, CHIPS)
    mine_a = spread(amp_a)
    other_a = swap(mine_a, "c")
    last_halves = halves(distant_blocks[2:])
    pieces_b = scatter(after(added([middle_halves, last_halves]), mine_a))
    sums = [[gamma(side, store, near_blocks, mine_a, other_a) for store in range(2)] for side in range(2)]
    amp_b = amplitudes(distant, after(pieces_b, sums), CHIPS)
    mine_b = spread(amp_b)
    other_b = swap(mine_b, "c")
    there = [gamma(side, 1, distant_blocks, mine_b, other_b, sums[side][1], BF16) for side in range(2)]
    arrived = [swap(part, "yh").astype(F32) for part in there]
    mine_b, other_b = after((mine_b, other_b), there)
    here = [gamma(side, 0, distant_blocks, mine_b, other_b, sums[side][0]) for side in range(2)]
    gamma_own, gamma_partner = (here[side] + arrived[side] for side in range(2))
    return gamma_own, gamma_partner[None]


def solution(mesh):
    grid = Mesh(mesh.devices.reshape(SIZES), AXES)
    aux, virt = ("x", "yl", "c"), ("z", "yh")
    in_specs = (P(aux, virt), P(None, aux, virt), P(), P())
    out_specs = (P(aux, virt), P(None, aux, virt))
    return jax.shard_map(local, mesh=grid, in_specs=in_specs, out_specs=out_specs, check_vma=False)
```

```python
import functools

import jax
import jax.numpy as jnp
from jax import lax
from jax.experimental import pallas as pl
from jax.experimental.pallas import tpu as pltpu
from jax.sharding import Mesh, PartitionSpec as P

AXES = ("x", "yl", "c", "z", "yh")
SIZES = (4, 2, 2, 8, 2)
NZ = 8
CHIPS = 8
F32, BF16 = jnp.float32, jnp.bfloat16


def shift(value, axis, size, step):
    return lax.ppermute(value, axis, [(i, (i + step) % size) for i in range(size)])


def swap(value, axis):
    return lax.ppermute(value, axis, [(0, 1), (1, 0)])


class Lazy:
    def __init__(self, scratch, copy):
        self.scratch, self.copy = scratch, copy

    def get(self):
        if self.copy is not None:
            self.copy.wait()
            self.copy = None
        return self.scratch


def call(kernel, out_shape, *args, scalar=False, cost=0):
    lead = 1 if scalar else 0
    windows = [arg[1] if isinstance(arg, tuple) else None for arg in args[lead:]]
    args = [arg[0] if isinstance(arg, tuple) else arg for arg in args]
    moved = args[lead:]
    count = len(moved)
    outs = len(jax.tree.leaves(out_shape))

    def body(*refs):
        sources = refs[lead:lead + count]
        targets = refs[lead + count:lead + count + outs]
        scratch = refs[lead + count + outs:-1]
        sems = refs[-1]
        lazy = []
        for index in range(count):
            source = sources[index]
            if windows[index] is not None:
                source = source.at[:, windows[index]]
            copy = pltpu.make_async_copy(source, scratch[index], sems.at[index])
            copy.start()
            lazy.append(Lazy(scratch[index], copy))
        kernel(*refs[:lead], *lazy, *targets)
        for item in lazy:
            item.get()

    buffers = []
    for arg, window in zip(moved, windows):
        shape = arg.shape if window is None else (arg.shape[0], window.stop - window.start)
        buffers.append(pltpu.VMEM(shape, arg.dtype))
    specs = [pl.BlockSpec(memory_space=pltpu.SMEM)] * lead + [pl.BlockSpec(memory_space=pltpu.HBM)] * count
    out_specs = jax.tree.map(lambda _: pl.BlockSpec(memory_space=pltpu.VMEM), out_shape)
    return pl.pallas_call(
        body,
        out_shape=out_shape,
        in_specs=specs,
        out_specs=out_specs,
        scratch_shapes=buffers + [pltpu.SemaphoreType.DMA((count,))],
        cost_estimate=pl.CostEstimate(flops=cost, bytes_accessed=0, transcendentals=0),
        compiler_params=pltpu.CompilerParams(vmem_limit_bytes=56 * 1024 * 1024),
    )(*args)


def prepare_kernel(width, core, *refs):
    out = refs[-1]
    parts = [ref.get() for ref in refs[:-1]]
    count = len(parts) // 2
    zero = core[0] == 0
    start = 0
    for index in range(count):
        here, peer = parts[index], parts[count + index]
        rows = here.shape[0]
        for side in range(2):
            columns = slice(side * width, (side + 1) * width)
            first, second = here[:, columns].T, peer[:, columns].T
            into = slice(start, start + rows)
            out[2 * side * width:(2 * side + 1) * width, into] = jnp.where(zero, first, second)
            out[(2 * side + 1) * width:(2 * side + 2) * width, into] = jnp.where(zero, second, first)
        start += rows


def products_kernel(counts, width, *refs):
    left = refs[0].get()
    kept, given = refs[-1 - len(counts)], refs[-len(counts):]
    position = 1
    for index, count in enumerate(counts):
        parts = [ref.get() for ref in refs[position:position + count]]
        position += count
        for side in range(2):
            columns = slice(width, 2 * width) if side == 0 else slice(0, width)
            total = None
            start = 0
            for part in parts:
                rows = part.shape[0]
                value = jnp.dot(
                    left[2 * side * width:(2 * side + 2) * width, start:start + rows],
                    part[:, columns],
                    preferred_element_type=F32,
                )
                total = value if total is None else total + value
                start += rows
            place = slice((2 * index + side) * width, (2 * index + side + 1) * width)
            kept[:, place] = total[:width]
            given[index][:, side * width:(side + 1) * width] = total[width:]


def products(left, blocks, width, cost):
    counts = [len(block) for block in blocks]
    flat = [part for block in blocks for part in block]
    kept = jax.ShapeDtypeStruct((width, 2 * width * len(blocks)), F32)
    given = [jax.ShapeDtypeStruct((width, 2 * width), F32)] * len(blocks)
    kept, *given = call(functools.partial(products_kernel, counts, width), [kept, *given], left, *flat, cost=cost)
    return kept, given


def sum_kernel(counts, width, *refs):
    out = refs[-1]
    position = 0
    place = 0
    for count in counts:
        kept = refs[position].get()
        for index in range(count):
            columns = slice(index * 2 * width, (index + 1) * 2 * width)
            arrived = refs[position + 1 + index].get()
            out[:, place:place + 2 * width] = (kept[:, columns] + arrived[...]).astype(BF16)
            place += 2 * width
        position += count + 1


def amplitude_kernel(count, width, copies, pieces, row_level, col_energy, out):
    pieces, row_level, col_energy = pieces.get(), row_level.get(), col_energy.get()
    for index in range(count):
        denom = row_level[...] - col_energy[:, index * width:(index + 1) * width]
        direct = None
        crossed = None
        for chip in range(CHIPS):
            first = pieces[chip, :, (2 * index) * width:(2 * index + 1) * width].astype(F32)
            second = pieces[chip, :, (2 * index + 1) * width:(2 * index + 2) * width].astype(F32)
            direct = first if direct is None else direct + first
            crossed = second if crossed is None else crossed + second
        amp = ((2.0 * direct - crossed) / denom).astype(BF16)
        amp_crossed = ((2.0 * crossed - direct) / denom).astype(BF16)
        for copy in range(copies):
            out[copy, :, (2 * index) * width:(2 * index + 1) * width] = amp
            out[copy, :, (2 * index + 1) * width:(2 * index + 2) * width] = amp_crossed


def contract(block, amps):
    return lax.dot_general(block, amps, (((1,), (1,)), ((), ())), preferred_element_type=F32)


def gamma_kernel(counts, width, step, side, store, add, *refs):
    core, mine, other = refs[0], refs[1].get(), refs[2].get()
    count = len(counts)
    blocks = []
    position = 3
    for parts in counts:
        blocks.append([ref.get() for ref in refs[position:position + parts]])
        position += parts
    out = refs[-1]
    before = refs[position].get() if add else None
    zero = core[0] == 0
    chosen = zero if store == 0 else jnp.logical_not(zero)
    amps = []
    for index in range(count):
        place = slice((2 * index + side) * width, (2 * index + side + 1) * width)
        amps.append(jnp.where(chosen, mine[:, place], other[:, place]))
    for start in range(0, out.shape[0], step):
        into = slice(start, start + step)
        total = None
        for index, parts in enumerate(blocks):
            size = parts[0].shape[0]
            rows = slice(start % size, start % size + step)
            value = contract(parts[start // size][rows, :], amps[index])
            total = value if total is None else total + value
        if add:
            total = total + before[into, :]
        out[into, :] = total.astype(out.dtype)


def local(own, partner_blocks, occ_energy, virt_energy):
    x, yl, c, z, yh = (lax.axis_index(name) for name in AXES)
    k = x * 2 + yl
    depth, width = own.shape
    half = depth // 2
    rows = width // CHIPS
    step = half
    first = c == 0
    core = c.astype(jnp.int32).reshape(1)

    base = jnp.concatenate([own, partner_blocks[0]], axis=1)
    base = (base,)
    base_peer = (swap(base[0], "yh"),)
    shape = jax.ShapeDtypeStruct((4 * width, depth), BF16)
    left = call(functools.partial(prepare_kernel, width), shape, core, *base, *base_peer, scalar=True)
    level = occ_energy[0] + occ_energy[1]
    row_energy = lax.dynamic_slice_in_dim(virt_energy, (z * 2 + (yh ^ c)) * width + k * rows, rows)
    row_level = (level - row_energy)[:, None]
    by_block = virt_energy.reshape(NZ, 2, width)
    col_energy = {d: lax.dynamic_slice(by_block, ((z + d) % NZ, yh, 0), (1, 1, width)).reshape(1, width) for d in range(-3, 5)}

    def after(values, *others):
        return lax.optimization_barrier((values, others))[0]

    def halves(blocks, cost=0):
        kept, given = products(left, blocks, width, cost)
        return kept, [swap(part, "c") for part in given]

    def added(sets):
        counts = [len(given) for _, given in sets]
        shape = jax.ShapeDtypeStruct((width, 2 * width * sum(counts)), BF16)
        flat = [part for kept, given in sets for part in [kept, *given]]
        return call(functools.partial(sum_kernel, counts, width), shape, *flat)

    def scatter(summed):
        return lax.all_to_all(summed.reshape(CHIPS, rows, -1), ("x", "yl"), 0, 0, tiled=True)

    def amplitudes(group, pieces, copies):
        cols = jnp.concatenate([col_energy[d] for d in group], axis=1)
        shape = jax.ShapeDtypeStruct((copies, rows, 2 * width * len(group)), BF16)
        kernel = functools.partial(amplitude_kernel, len(group), width, copies)
        return call(kernel, shape, pieces, row_level, cols)

    def spread(copies):
        return lax.all_to_all(copies, ("x", "yl"), 0, 0, tiled=True).reshape(width, -1)

    def gamma(side, store, blocks, mine, other, before=None, dtype=F32):
        counts = [len(block) for block in blocks]
        kernel = functools.partial(gamma_kernel, counts, width, step, side, store, before is not None)
        columns = slice(width, 2 * width) if side == 0 else slice(0, width)
        flat = [(part, columns) for block in blocks for part in block]
        extra = [] if before is None else [before]
        return call(kernel, jax.ShapeDtypeStruct((depth, width), dtype), core, mine, other, *flat, *extra, scalar=True)

    def both(parts, way):
        return tuple(shift(part, "z", NZ, way) for part in parts)

    up1, down1 = both(base, 1), both(base, -1)
    up1, down1 = after((up1, down1), base_peer)
    up2, down2 = both(up1, 1), both(down1, -1)
    near, distant = (0, 1, -1), (2, -2, 3, -3, 4)
    near_blocks = [base, down1, up1]
    near_halves = halves(near_blocks)
    (up2, down2), near_halves = lax.optimization_barrier(((up2, down2), near_halves))
    up3, down3 = both(up2, 1), both(down2, -1)
    summed_a = added([near_halves])
    pieces_a = scatter(summed_a)
    middle_halves = halves(after([down2, up2], pieces_a))
    far = shift(up3[0][:half], "z", NZ, 1), shift(down3[0][half:], "z", NZ, -1)

    distant_blocks = [down2, up2, down3, up3, far]
    amp_a = amplitudes(near, after(pieces_a, up3, down3), CHIPS)
    mine_a = spread(amp_a)
    other_a = swap(mine_a, "c")
    last_halves = halves(distant_blocks[2:])
    pieces_b = scatter(after(added([after(middle_halves, far), last_halves]), mine_a))
    sums = [[gamma(side, store, near_blocks, mine_a, other_a) for store in range(2)] for side in range(2)]
    amp_b = amplitudes(distant, after(pieces_b, sums), CHIPS)
    mine_b = spread(amp_b)
    other_b = swap(mine_b, "c")
    there = [gamma(side, 1, distant_blocks, mine_b, other_b, sums[side][1], BF16) for side in range(2)]
    arrived = [swap(part, "yh").astype(F32) for part in there]
    mine_b, other_b = after((mine_b, other_b), there)
    here = [gamma(side, 0, distant_blocks, mine_b, other_b, sums[side][0]) for side in range(2)]
    gamma_own, gamma_partner = (here[side] + arrived[side] for side in range(2))
    return gamma_own, gamma_partner[None]


def solution(mesh):
    grid = Mesh(mesh.devices.reshape(SIZES), AXES)
    aux, virt = ("x", "yl", "c"), ("z", "yh")
    in_specs = (P(aux, virt), P(None, aux, virt), P(), P())
    out_specs = (P(aux, virt), P(None, aux, virt))
    return jax.shard_map(local, mesh=grid, in_specs=in_specs, out_specs=out_specs, check_vma=False)
```

```python
import functools

import jax
import jax.numpy as jnp
from jax import lax
from jax.experimental import pallas as pl
from jax.experimental.pallas import tpu as pltpu
from jax.sharding import Mesh, PartitionSpec as P

AXES = ("x", "yl", "c", "z", "yh")
SIZES = (4, 2, 2, 8, 2)
NZ = 8
CHIPS = 8
F32, BF16 = jnp.float32, jnp.bfloat16


def shift(value, axis, size, step):
    return lax.ppermute(value, axis, [(i, (i + step) % size) for i in range(size)])


def swap(value, axis):
    return lax.ppermute(value, axis, [(0, 1), (1, 0)])


class Lazy:
    def __init__(self, scratch, copy):
        self.scratch, self.copy = scratch, copy

    def get(self):
        if self.copy is not None:
            self.copy.wait()
            self.copy = None
        return self.scratch


def call(kernel, out_shape, *args, scalar=False, cost=0):
    lead = 1 if scalar else 0
    windows = [arg[1] if isinstance(arg, tuple) else None for arg in args[lead:]]
    args = [arg[0] if isinstance(arg, tuple) else arg for arg in args]
    moved = args[lead:]
    count = len(moved)
    outs = len(jax.tree.leaves(out_shape))

    def body(*refs):
        sources = refs[lead:lead + count]
        targets = refs[lead + count:lead + count + outs]
        scratch = refs[lead + count + outs:-1]
        sems = refs[-1]
        lazy = []
        for index in range(count):
            source = sources[index]
            if windows[index] is not None:
                source = source.at[:, windows[index]]
            copy = pltpu.make_async_copy(source, scratch[index], sems.at[index])
            copy.start()
            lazy.append(Lazy(scratch[index], copy))
        kernel(*refs[:lead], *lazy, *targets)
        for item in lazy:
            item.get()

    buffers = []
    for arg, window in zip(moved, windows):
        shape = arg.shape if window is None else (arg.shape[0], window.stop - window.start)
        buffers.append(pltpu.VMEM(shape, arg.dtype))
    specs = [pl.BlockSpec(memory_space=pltpu.SMEM)] * lead + [pl.BlockSpec(memory_space=pltpu.HBM)] * count
    out_specs = jax.tree.map(lambda _: pl.BlockSpec(memory_space=pltpu.VMEM), out_shape)
    return pl.pallas_call(
        body,
        out_shape=out_shape,
        in_specs=specs,
        out_specs=out_specs,
        scratch_shapes=buffers + [pltpu.SemaphoreType.DMA((count,))],
        cost_estimate=pl.CostEstimate(flops=cost, bytes_accessed=0, transcendentals=0),
        compiler_params=pltpu.CompilerParams(vmem_limit_bytes=56 * 1024 * 1024),
    )(*args)


def prepare_kernel(width, core, *refs):
    out = refs[-1]
    parts = [ref.get() for ref in refs[:-1]]
    count = len(parts) // 2
    zero = core[0] == 0
    start = 0
    for index in range(count):
        here, peer = parts[index], parts[count + index]
        rows = here.shape[0]
        for side in range(2):
            columns = slice(side * width, (side + 1) * width)
            first, second = here[:, columns].T, peer[:, columns].T
            into = slice(start, start + rows)
            out[2 * side * width:(2 * side + 1) * width, into] = jnp.where(zero, first, second)
            out[(2 * side + 1) * width:(2 * side + 2) * width, into] = jnp.where(zero, second, first)
        start += rows


def products_kernel(counts, width, *refs):
    left = refs[0].get()
    kept, given = refs[-1 - len(counts)], refs[-len(counts):]
    position = 1
    for index, count in enumerate(counts):
        parts = [ref.get() for ref in refs[position:position + count]]
        position += count
        for side in range(2):
            columns = slice(width, 2 * width) if side == 0 else slice(0, width)
            total = None
            start = 0
            for part in parts:
                rows = part.shape[0]
                value = jnp.dot(
                    left[2 * side * width:(2 * side + 2) * width, start:start + rows],
                    part[:, columns],
                    preferred_element_type=F32,
                )
                total = value if total is None else total + value
                start += rows
            place = slice((2 * index + side) * width, (2 * index + side + 1) * width)
            kept[:, place] = total[:width]
            given[index][:, side * width:(side + 1) * width] = total[width:]


def products(left, blocks, width, cost):
    counts = [len(block) for block in blocks]
    flat = [part for block in blocks for part in block]
    kept = jax.ShapeDtypeStruct((width, 2 * width * len(blocks)), F32)
    given = [jax.ShapeDtypeStruct((width, 2 * width), F32)] * len(blocks)
    kept, *given = call(functools.partial(products_kernel, counts, width), [kept, *given], left, *flat, cost=cost)
    return kept, given


def sum_kernel(counts, width, *refs):
    out = refs[-1]
    position = 0
    place = 0
    for count in counts:
        kept = refs[position].get()
        for index in range(count):
            columns = slice(index * 2 * width, (index + 1) * 2 * width)
            arrived = refs[position + 1 + index].get()
            out[:, place:place + 2 * width] = (kept[:, columns] + arrived[...]).astype(BF16)
            place += 2 * width
        position += count + 1


def amplitude_kernel(count, width, copies, pieces, row_level, col_energy, out):
    pieces, row_level, col_energy = pieces.get(), row_level.get(), col_energy.get()
    for index in range(count):
        denom = row_level[...] - col_energy[:, index * width:(index + 1) * width]
        direct = None
        crossed = None
        for chip in range(CHIPS):
            first = pieces[chip, :, (2 * index) * width:(2 * index + 1) * width].astype(F32)
            second = pieces[chip, :, (2 * index + 1) * width:(2 * index + 2) * width].astype(F32)
            direct = first if direct is None else direct + first
            crossed = second if crossed is None else crossed + second
        amp = ((2.0 * direct - crossed) / denom).astype(BF16)
        amp_crossed = ((2.0 * crossed - direct) / denom).astype(BF16)
        for copy in range(copies):
            out[copy, :, (2 * index) * width:(2 * index + 1) * width] = amp
            out[copy, :, (2 * index + 1) * width:(2 * index + 2) * width] = amp_crossed


def contract(block, amps):
    return lax.dot_general(block, amps, (((1,), (1,)), ((), ())), preferred_element_type=F32)


def gamma_kernel(counts, width, step, side, store, add, *refs):
    core, mine, other = refs[0], refs[1].get(), refs[2].get()
    count = len(counts)
    blocks = []
    position = 3
    for parts in counts:
        blocks.append([ref.get() for ref in refs[position:position + parts]])
        position += parts
    out = refs[-1]
    before = refs[position].get() if add else None
    zero = core[0] == 0
    chosen = zero if store == 0 else jnp.logical_not(zero)
    amps = []
    for index in range(count):
        place = slice((2 * index + side) * width, (2 * index + side + 1) * width)
        amps.append(jnp.where(chosen, mine[:, place], other[:, place]))
    for start in range(0, out.shape[0], step):
        into = slice(start, start + step)
        total = None
        for index, parts in enumerate(blocks):
            size = parts[0].shape[0]
            rows = slice(start % size, start % size + step)
            value = contract(parts[start // size][rows, :], amps[index])
            total = value if total is None else total + value
        if add:
            total = total + before[into, :]
        out[into, :] = total.astype(out.dtype)


def local(own, partner_blocks, occ_energy, virt_energy):
    x, yl, c, z, yh = (lax.axis_index(name) for name in AXES)
    k = x * 2 + yl
    depth, width = own.shape
    half = depth // 2
    rows = width // CHIPS
    step = half
    first = c == 0
    core = c.astype(jnp.int32).reshape(1)

    base = jnp.concatenate([own, partner_blocks[0]], axis=1)
    base = (base,)
    base_peer = (swap(base[0], "yh"),)
    shape = jax.ShapeDtypeStruct((4 * width, depth), BF16)
    left = call(functools.partial(prepare_kernel, width), shape, core, *base, *base_peer, scalar=True)
    level = occ_energy[0] + occ_energy[1]
    row_energy = lax.dynamic_slice_in_dim(virt_energy, (z * 2 + (yh ^ c)) * width + k * rows, rows)
    row_level = (level - row_energy)[:, None]
    by_block = virt_energy.reshape(NZ, 2, width)
    col_energy = {d: lax.dynamic_slice(by_block, ((z + d) % NZ, yh, 0), (1, 1, width)).reshape(1, width) for d in range(-3, 5)}

    def after(values, *others):
        return lax.optimization_barrier((values, others))[0]

    def halves(blocks, cost=0):
        kept, given = products(left, blocks, width, cost)
        return kept, [swap(part, "c") for part in given]

    def added(sets):
        counts = [len(given) for _, given in sets]
        shape = jax.ShapeDtypeStruct((width, 2 * width * sum(counts)), BF16)
        flat = [part for kept, given in sets for part in [kept, *given]]
        return call(functools.partial(sum_kernel, counts, width), shape, *flat)

    def scatter(summed):
        return lax.all_to_all(summed.reshape(CHIPS, rows, -1), ("x", "yl"), 0, 0, tiled=True)

    def amplitudes(group, pieces, copies):
        cols = jnp.concatenate([col_energy[d] for d in group], axis=1)
        shape = jax.ShapeDtypeStruct((copies, rows, 2 * width * len(group)), BF16)
        kernel = functools.partial(amplitude_kernel, len(group), width, copies)
        return call(kernel, shape, pieces, row_level, cols)

    def spread(copies):
        return lax.all_to_all(copies, ("x", "yl"), 0, 0, tiled=True).reshape(width, -1)

    def gamma(side, store, blocks, mine, other, before=None, dtype=F32):
        counts = [len(block) for block in blocks]
        kernel = functools.partial(gamma_kernel, counts, width, step, side, store, before is not None)
        columns = slice(width, 2 * width) if side == 0 else slice(0, width)
        flat = [(part, columns) for block in blocks for part in block]
        extra = [] if before is None else [before]
        return call(kernel, jax.ShapeDtypeStruct((depth, width), dtype), core, mine, other, *flat, *extra, scalar=True)

    def both(parts, way):
        return tuple(shift(part, "z", NZ, way) for part in parts)

    up1, down1 = both(base, 1), both(base, -1)
    up1, down1 = after((up1, down1), base_peer)
    up2, down2 = both(up1, 1), both(down1, -1)
    near, distant = (0, 1, -1, 2, -2), (3, -3, 4)
    near_blocks = [base, down1, up1]
    near_halves = halves(near_blocks)
    (up2, down2), near_halves = lax.optimization_barrier(((up2, down2), near_halves))
    up3, down3 = both(up2, 1), both(down2, -1)
    middle_halves = halves([down2, up2])
    up3, down3 = after((up3, down3), middle_halves)
    pieces_a = scatter(added([near_halves, middle_halves]))
    far = shift(up3[0][:half], "z", NZ, 1), shift(down3[0][half:], "z", NZ, -1)

    near_blocks = near_blocks + [down2, up2]
    distant_blocks = [down3, up3, far]
    amp_a = amplitudes(near, pieces_a, CHIPS)
    mine_a = spread(amp_a)
    other_a = swap(mine_a, "c")
    last_halves = halves(distant_blocks)
    pieces_b = scatter(after(added([last_halves]), mine_a))
    sums = [[gamma(side, store, near_blocks, mine_a, other_a) for store in range(2)] for side in range(2)]
    amp_b = amplitudes(distant, after(pieces_b, sums[0]), CHIPS)
    mine_b = spread(amp_b)
    other_b = swap(after(mine_b, sums[1]), "c")
    there = [gamma(side, 1, distant_blocks, mine_b, other_b, sums[side][1], BF16) for side in range(2)]
    arrived = [swap(part, "yh").astype(F32) for part in there]
    mine_b, other_b = after((mine_b, other_b), there)
    here = [gamma(side, 0, distant_blocks, mine_b, other_b, sums[side][0]) for side in range(2)]
    gamma_own, gamma_partner = (here[side] + arrived[side] for side in range(2))
    return gamma_own, gamma_partner[None]


def solution(mesh):
    grid = Mesh(mesh.devices.reshape(SIZES), AXES)
    aux, virt = ("x", "yl", "c"), ("z", "yh")
    in_specs = (P(aux, virt), P(None, aux, virt), P(), P())
    out_specs = (P(aux, virt), P(None, aux, virt))
    return jax.shard_map(local, mesh=grid, in_specs=in_specs, out_specs=out_specs, check_vma=False)
```
